32 devices in a mesh: island: 16 (over z, y, x), fsdp: 2 (over core).
Axes of the slice: x: 2, y: 2, z: 4, core: 2. Of those that a mesh axis runs over, the one named last changes fastest.
Arguments:
- global_weights: float32 [4, 64, 8192], P(None, 'fsdp'), may hold values from -6 to 6
- local_weights: float32 [16, 4, 64, 8192], P('island', None, 'fsdp'), may hold values from -6 to 6
- momentum: float32 [4, 64, 8192], P(None, 'fsdp', 'island'), may hold values from -4 to 4
Outputs:
- new_global: float32 [4, 64, 8192], P(None, 'fsdp')
- new_momentum: float32 [4, 64, 8192], P(None, 'fsdp', 'island')
The draws below stay inside these ranges and needn't reach their ends.
All inputs are finite; a program needn't handle non-finite values.
Results may differ from the reference program's by a relative error of at most 0.00002.
Values sent between devices are 32-bit elements; how exact they have to be, the bound alone decides.
A program may use at most 64 MiB of HBM per device.

```python
import jax
import jax.numpy as jnp
from jax import lax

D = 8192
LAYERS = 4
ROWS = 64
ISLANDS = 16


def with_spikes(values, rng, source, target, blocks, factor):
    owner, partner = [(jnp.arange(values.shape[dim]) // (values.shape[dim] // blocks)).reshape([-1 if axis == dim else 1 for axis in range(values.ndim)]) for dim in (source, target)]
    chosen = jax.random.permutation(rng, blocks)[partner]
    strong = (owner == chosen) | (owner == (partner + blocks // 2) % blocks)
    return jnp.where(strong, factor * values, values)


def steps_of(stream_key, shape, cuts, smallest, high):
    loudness = 1.0
    for position, shards_of in cuts:
        draws = jax.random.uniform(jax.random.fold_in(jax.random.fold_in(stream_key, 6), position), (shards_of,), jnp.float32, smallest / len(cuts), high / len(cuts))
        loudness = loudness * jnp.repeat(jnp.exp(draws), shape[position] // shards_of).reshape((-1,) + (1,) * (len(shape) - 1 - position))
    return loudness


def centred(key, shape, deviation, limit, pieces=(), dtype=jnp.bfloat16):
    factor_of = steps_of(key, shape, pieces, -0.22, 0.18) if pieces else 1.0
    drawn = jax.random.normal(key, shape, jnp.float32) * deviation * factor_of
    return jnp.minimum(jnp.maximum(drawn, -limit), limit).astype(dtype)


def gaussian_with(rng, extent, width, reach, cuts, heavy, held_as=jnp.bfloat16):
    entries = width * jax.random.normal(rng, extent, jnp.float32)
    if cuts:
        entries = entries * steps_of(rng, extent, cuts, -0.22, 0.18)
    return jnp.clip(with_spikes(entries, jax.random.fold_in(rng, 3), *heavy), -reach, reach).astype(held_as)


def setup_inputs(seed: int = 0) -> dict:
    key_of = jax.random.split(jax.random.key(seed), 4)
    global_weights = centred(key_of[0], (LAYERS, ROWS, D), 1.0, 6.0, ((1, 2),), jnp.float32)
    local_weights = gaussian_with(key_of[1], (ISLANDS, LAYERS, ROWS, D), 1.0, 6.0, ((0, 16), (2, 2)), (0, 3, 16, 2.0), jnp.float32)
    momentum = centred(key_of[2], (LAYERS, ROWS, D), 0.3, 4.0, ((1, 2), (2, 16)), jnp.float32)
    return dict(global_weights=global_weights, local_weights=local_weights, momentum=momentum)


NESTEROV = 0.9
OUTER_RATE = 0.7


def reference(global_weights, local_weights, momentum):
    def accumulate(total, local_one):
        return total + (global_weights - local_one), None

    summed, _ = lax.scan(accumulate, jnp.zeros_like(global_weights), local_weights)
    outer_grad = summed / ISLANDS
    new_momentum = NESTEROV * momentum + outer_grad
    new_global = global_weights - OUTER_RATE * (outer_grad + NESTEROV * new_momentum)
    return new_global, new_momentum
```

```python
import functools

import jax
import jax.numpy as jnp
from jax import lax
from jax.experimental import pallas as pl
from jax.experimental.pallas import tpu as pltpu
from jax.sharding import PartitionSpec as P

NESTEROV = 0.9
OUTER_RATE = 0.7
LANES = 128
SUBLANES = 8


def grid_of(islands):
    return {16: (4, 2, 2), 64: (8, 8)}.get(islands, (islands,))


def plan(dims, groups):
    if len(dims) == 3:
        z, y, x = 0, 1, 2
        wish = [((z, y, x), 2), ((x, y, z), 3), ((y, x, z), 3),
                ((z, x, y), 2), ((x, y, z), 2), ((y, x, z), 2), ((z, y, x), 2)]
    elif len(dims) == 2:
        wish = [((0, 1), 1), ((1, 0), 1)]
    else:
        wish = [((0,), 1)]
    total = sum(share for _, share in wish)
    streams, at, seen = [], 0, 0
    for order, share in wish:
        seen += share
        end = groups * seen // total
        if end > at:
            streams.append((order, at, end - at))
        at = end
    return streams


def phase_slots(n):
    return 1 if n == 2 else 2 * (n - 1)


def kernel(dims, streams, n_sems, g_hbm, l_hbm, m_hbm, out_hbm, nm_hbm,
           gw, lw, mom, acc, gath, nm, landing, send_sem, recv_sem, in_sem, out_sem):
    axes = range(len(dims))
    me = lax.axis_index("island")
    strides = []
    for a in axes:
        stride = 1
        for b in dims[a + 1:]:
            stride *= b
        strides.append(stride)
    pos = [(me // strides[a]) % dims[a] for a in axes]
    islands = strides[0] * dims[0]

    loads = []
    for j, (_, g0, ng) in enumerate(streams):
        rows = pl.ds(g0, ng)
        loads.append([
            pltpu.make_async_copy(g_hbm.at[rows], gw.at[rows], in_sem.at[3 * j]),
            pltpu.make_async_copy(l_hbm.at[rows], lw.at[rows], in_sem.at[3 * j + 1]),
            pltpu.make_async_copy(m_hbm.at[rows], mom.at[rows], in_sem.at[3 * j + 2]),
        ])
        for load in loads[-1][:2]:
            load.start()
    for load in loads:
        load[2].start()

    barrier = pltpu.get_barrier_semaphore()
    for a in axes:
        for step, there in ((1, pos[a] < dims[a] - 1), (-1, pos[a] > 0)):
            @pl.when(there)
            def _():
                pl.semaphore_signal(barrier, inc=1,
                                    device_id={"island": me + step * strides[a]},
                                    device_id_type=pl.DeviceIdType.MESH)

    counter = iter(range(n_sems))
    ends = []

    def remote(src, dst, sem, axis, step):
        return pltpu.make_async_remote_copy(
            src_ref=src, dst_ref=dst, send_sem=send_sem.at[sem],
            recv_sem=recv_sem.at[sem],
            device_id={"island": me + step * strides[axis]},
            device_id_type=pl.DeviceIdType.MESH)

    def part(ref, rows, fixed):
        return ref.at[(rows,) + tuple(fixed.get(a, slice(None)) for a in axes)]

    def stream(j):
        order, g0, ng = streams[j]
        rows = pl.ds(g0, ng)
        loads[j][0].wait()
        loads[j][1].wait()
        acc[rows] = gw[rows] - lw[rows]
        yield
        fixed = {}
        for phase, a in enumerate(order):
            n, p = dims[a], pos[a]
            land = landing[j * len(dims) + phase]
            sems = [[next(counter) for _ in range(n - 1)] for _ in range(2)]

            def slot(side, k, land=land, n=n):
                return land.at[0 if n == 2 else side * (n - 1) + k]

            def mine(s, a=a, fixed=dict(fixed)):
                return part(acc, rows, {**fixed, a: s})

            def take(side, k, s):
                block = mine(s)
                remote(block, slot(side, k), sems[side][k], a, 1 - 2 * side).wait_recv()
                block[...] = block[...] + slot(side, k)[...]

            for k in range(n - 1):
                for side in range(2):
                    lead = p if side == 0 else n - 1 - p
                    s = n - 1 - k + p if side == 0 else k - lead

                    @pl.when(lead <= k)
                    def _():
                        if k > 0:
                            @pl.when(lead > 0)
                            def _():
                                take(side, k - 1, s)
                        remote(mine(s), slot(side, k), sems[side][k], a,
                               1 - 2 * side).start()

                    def end(lead=lead, k=k, side=side, s=s, a=a,
                            mine=mine, slot=slot, sems=sems):
                        @pl.when(lead <= k)
                        def _():
                            remote(mine(s), slot(side, k), sems[side][k], a,
                                   1 - 2 * side).wait_send()
                    ends.append(end)
                yield
            for side in range(2):
                @pl.when((p if side == 0 else n - 1 - p) > 0)
                def _():
                    take(side, n - 2, p)
            fixed[a] = p

        own = (rows,) + tuple(pos)
        loads[j][2].wait()
        outer = acc[own] / islands
        moment = NESTEROV * mom[rows] + outer
        nm[rows] = moment
        gath[own] = gw[own] - OUTER_RATE * (outer + NESTEROV * moment)
        save = pltpu.make_async_copy(nm.at[rows], nm_hbm.at[rows], out_sem.at[2 * j])
        save.start()
        ends.append(save.wait)

        for a in reversed(order):
            n, p = dims[a], pos[a]
            del fixed[a]
            sems = [[next(counter) for _ in range(n - 1)] for _ in range(2)]

            def block_of(s, a=a, fixed=dict(fixed)):
                return part(gath, rows, {**fixed, a: s})

            for k in range(n):
                for side in range(2):
                    step = 1 - 2 * side
                    lead = p if side == 0 else n - 1 - p
                    s = p - step * k

                    @pl.when(k <= lead)
                    def _():
                        block = block_of(s)
                        if k > 0:
                            remote(block, block, sems[side][k - 1], a, step).wait_recv()
                        if k < n - 1:
                            @pl.when(lead < n - 1)
                            def _():
                                remote(block, block, sems[side][k], a, step).start()

                    if k < n - 1:
                        def end(k=k, lead=lead, n=n, s=s, side=side, step=step, a=a,
                                block_of=block_of, sems=sems):
                            @pl.when((k <= lead) & (lead < n - 1))
                            def _():
                                block = block_of(s)
                                remote(block, block, sems[side][k], a, step).wait_send()
                        ends.append(end)
                if k < n - 1:
                    yield
        store = pltpu.make_async_copy(gath.at[rows], out_hbm.at[rows], out_sem.at[2 * j + 1])
        store.start()
        ends.append(store.wait)

    running = [stream(j) for j in range(len(streams))]
    first = True
    while running:
        for one in list(running):
            if next(one, "end") == "end":
                running.remove(one)
            elif first:
                first = False
                peers = sum((pos[a] < dims[a] - 1).astype(jnp.int32)
                            + (pos[a] > 0).astype(jnp.int32) for a in axes)
                pl.semaphore_wait(barrier, peers)
    for end in ends:
        end()


def body(dims, global_weights, local_weights, momentum):
    layers, rows, width = global_weights.shape
    islands = lax.axis_size("island")
    cols = momentum.shape[2]
    groups = layers * rows // SUBLANES
    tiles = cols // LANES

    def to_tiles(array):
        array = array.reshape(groups, SUBLANES, -1, LANES)
        return array.transpose(0, 2, 1, 3)

    def from_tiles(array, like):
        array = array.reshape(groups, -1, SUBLANES, LANES)
        return array.transpose(0, 2, 1, 3).reshape(like.shape)

    wide = (groups,) + dims + (tiles, SUBLANES, LANES)
    narrow = (groups, tiles, SUBLANES, LANES)
    streams = plan(dims, groups)
    landings = []
    for order, _, ng in streams:
        left = dict(enumerate(dims))
        for a in order:
            n = left.pop(a)
            landings.append(pltpu.VMEM(
                (phase_slots(n), ng) + tuple(left[b] for b in sorted(left))
                + (tiles, SUBLANES, LANES), jnp.float32))
    n_sems = len(streams) * 4 * sum(n - 1 for n in dims)
    f32 = jnp.float32
    new_global, new_momentum = pl.pallas_call(
        functools.partial(kernel, dims, streams, n_sems),
        out_shape=(jax.ShapeDtypeStruct(wide, f32), jax.ShapeDtypeStruct(narrow, f32)),
        in_specs=[pl.BlockSpec(memory_space=pl.ANY)] * 3,
        out_specs=(pl.BlockSpec(memory_space=pl.ANY),) * 2,
        scratch_shapes=[
            pltpu.VMEM(wide, f32), pltpu.VMEM(wide, f32), pltpu.VMEM(narrow, f32),
            pltpu.VMEM(wide, f32), pltpu.VMEM(wide, f32), pltpu.VMEM(narrow, f32),
            landings,
            pltpu.SemaphoreType.DMA((n_sems,)), pltpu.SemaphoreType.DMA((n_sems,)),
            pltpu.SemaphoreType.DMA((3 * len(streams),)),
            pltpu.SemaphoreType.DMA((2 * len(streams),)),
        ],
        compiler_params=pltpu.CompilerParams(
            collective_id=0, has_side_effects=True, vmem_limit_bytes=40 * 2**20),
    )(
        to_tiles(global_weights).reshape(wide),
        to_tiles(local_weights[0]).reshape(wide),
        to_tiles(momentum),
    )
    return from_tiles(new_global, global_weights), from_tiles(new_momentum, momentum)


def solution(mesh):
    dims = grid_of(mesh.shape["island"])
    return jax.shard_map(
        functools.partial(body, dims),
        mesh=mesh,
        in_specs=(
            P(None, "fsdp", None),
            P("island", None, "fsdp", None),
            P(None, "fsdp", "island"),
        ),
        out_specs=(P(None, "fsdp", None), P(None, "fsdp", "island")),
        check_vma=False,
    )
```

```python
import functools

import jax
import jax.numpy as jnp
from jax import lax
from jax.experimental import pallas as pl
from jax.experimental.pallas import tpu as pltpu
from jax.sharding import PartitionSpec as P

NESTEROV = 0.9
OUTER_RATE = 0.7
ORDER = [2, 2, 1, 1, 0, 3, 3, 5, 3, 0, 3, 0, 4, 0, 3, 2, 1, 5, 3, 4, 3, 0, 0, 2, 1, 2, 0, 3, 2, 1, 1, 2, 0, 1, 2, 2, 4, 5, 1, 1, 2, 2, 1, 1, 2, 2, 1, 0, 1, 4, 2, 5, 2, 4, 5, 3, 1, 1, 0, 4, 3, 2, 4, 1, 5, 5, 4, 4, 5, 5, 0, 3, 4, 4, 5, 5, 4, 1, 2, 4, 5, 4, 5, 3, 3, 5, 5, 0, 3, 5, 4, 4, 0, 3, 1, 3, 3, 5, 4, 0, 0, 0, 0, 2, 0, 3, 5, 4]
LANES = 128
SUBLANES = 8


def grid_of(islands):
    return {16: (4, 2, 2), 64: (8, 8)}.get(islands, (islands,))


def plan(dims, groups):
    if len(dims) == 3:
        z, y, x = 0, 1, 2
        wish = [((0, 1, 2), 2), ((2, 1, 0), 3), ((1, 2, 0), 3), ((0, 2, 1), 2), ((2, 1, 0), 3), ((1, 2, 0), 3)]
    elif len(dims) == 2:
        wish = [((0, 1), 1), ((1, 0), 1)]
    else:
        wish = [((0,), 1)]
    total = sum(share for _, share in wish)
    streams, at, seen = [], 0, 0
    for order, share in wish:
        seen += share
        end = groups * seen // total
        if end > at:
            streams.append((order, at, end - at))
        at = end
    return streams


def turns(dims, n_streams):
    if ORDER is not None and len(dims) == 3:
        return ORDER
    steps = 2 + 2 * sum(1 if n == 2 else 2 * (n - 1) for n in dims)
    return [j for _ in range(steps) for j in range(n_streams)]


def phase_slots(n):
    return 1 if n == 2 else 2 * (n - 1)


def kernel(dims, streams, n_sems, g_hbm, l_hbm, m_hbm, out_hbm, nm_hbm,
           gw, lw, mom, acc, gath, nm, landing, send_sem, recv_sem, in_sem, out_sem):
    axes = range(len(dims))
    me = lax.axis_index("island")
    strides = []
    for a in axes:
        stride = 1
        for b in dims[a + 1:]:
            stride *= b
        strides.append(stride)
    pos = [(me // strides[a]) % dims[a] for a in axes]
    islands = strides[0] * dims[0]

    loads = []
    for j, (_, g0, ng) in enumerate(streams):
        rows = pl.ds(g0, ng)
        loads.append([
            pltpu.make_async_copy(g_hbm.at[rows], gw.at[rows], in_sem.at[3 * j]),
            pltpu.make_async_copy(l_hbm.at[rows], lw.at[rows], in_sem.at[3 * j + 1]),
            pltpu.make_async_copy(m_hbm.at[rows], mom.at[rows], in_sem.at[3 * j + 2]),
        ])
        for load in loads[-1][:2]:
            load.start()
    for load in loads:
        load[2].start()

    barrier = pltpu.get_barrier_semaphore()
    for a in axes:
        for step, there in ((1, pos[a] < dims[a] - 1), (-1, pos[a] > 0)):
            @pl.when(there)
            def _():
                pl.semaphore_signal(barrier, inc=1,
                                    device_id={"island": me + step * strides[a]},
                                    device_id_type=pl.DeviceIdType.MESH)

    counter = iter(range(n_sems))
    ends = []

    def remote(src, dst, sem, axis, step):
        return pltpu.make_async_remote_copy(
            src_ref=src, dst_ref=dst, send_sem=send_sem.at[sem],
            recv_sem=recv_sem.at[sem],
            device_id={"island": me + step * strides[axis]},
            device_id_type=pl.DeviceIdType.MESH)

    def part(ref, rows, fixed):
        return ref.at[(rows,) + tuple(fixed.get(a, slice(None)) for a in axes)]

    def stream(j):
        order, g0, ng = streams[j]
        rows = pl.ds(g0, ng)
        loads[j][0].wait()
        loads[j][1].wait()
        acc[rows] = gw[rows] - lw[rows]
        yield
        fixed = {}
        for phase, a in enumerate(order):
            n, p = dims[a], pos[a]
            land = landing[j * len(dims) + phase]
            sems = [[next(counter) for _ in range(n - 1)] for _ in range(2)]

            def slot(side, k, land=land, n=n):
                return land.at[0 if n == 2 else side * (n - 1) + k]

            def mine(s, a=a, fixed=dict(fixed)):
                return part(acc, rows, {**fixed, a: s})

            def take(side, k, s):
                block = mine(s)
                remote(block, slot(side, k), sems[side][k], a, 1 - 2 * side).wait_recv()
                block[...] = block[...] + slot(side, k)[...]

            for k in range(n - 1):
                for side in range(2):
                    lead = p if side == 0 else n - 1 - p
                    s = n - 1 - k + p if side == 0 else k - lead

                    @pl.when(lead <= k)
                    def _():
                        if k > 0:
                            @pl.when(lead > 0)
                            def _():
                                take(side, k - 1, s)
                        remote(mine(s), slot(side, k), sems[side][k], a,
                               1 - 2 * side).start()

                    def end(lead=lead, k=k, side=side, s=s, a=a,
                            mine=mine, slot=slot, sems=sems):
                        @pl.when(lead <= k)
                        def _():
                            remote(mine(s), slot(side, k), sems[side][k], a,
                                   1 - 2 * side).wait_send()
                    ends.append(end)
                    if n > 2 or side == 1:
                        yield
            for side in range(2):
                @pl.when((p if side == 0 else n - 1 - p) > 0)
                def _():
                    take(side, n - 2, p)
            fixed[a] = p

        own = (rows,) + tuple(pos)
        loads[j][2].wait()
        outer = acc[own] / islands
        moment = NESTEROV * mom[rows] + outer
        nm[rows] = moment
        gath[own] = gw[own] - OUTER_RATE * (outer + NESTEROV * moment)
        save = pltpu.make_async_copy(nm.at[rows], nm_hbm.at[rows], out_sem.at[2 * j])
        save.start()
        ends.append(save.wait)

        for a in reversed(order):
            n, p = dims[a], pos[a]
            del fixed[a]
            sems = [[next(counter) for _ in range(n - 1)] for _ in range(2)]

            def block_of(s, a=a, fixed=dict(fixed)):
                return part(gath, rows, {**fixed, a: s})

            for k in range(n):
                for side in range(2):
                    step = 1 - 2 * side
                    lead = p if side == 0 else n - 1 - p
                    s = p - step * k

                    @pl.when(k <= lead)
                    def _():
                        block = block_of(s)
                        if k > 0:
                            remote(block, block, sems[side][k - 1], a, step).wait_recv()
                        if k < n - 1:
                            @pl.when(lead < n - 1)
                            def _():
                                remote(block, block, sems[side][k], a, step).start()

                    if k < n - 1:
                        def end(k=k, lead=lead, n=n, s=s, side=side, step=step, a=a,
                                block_of=block_of, sems=sems):
                            @pl.when((k <= lead) & (lead < n - 1))
                            def _():
                                block = block_of(s)
                                remote(block, block, sems[side][k], a, step).wait_send()
                        ends.append(end)
                        if n > 2 or side == 1:
                            yield
        store = pltpu.make_async_copy(gath.at[rows], out_hbm.at[rows], out_sem.at[2 * j + 1])
        store.start()
        ends.append(store.wait)

    running = [stream(j) for j in range(len(streams))]
    greeted = False
    began = set()
    for j in turns(dims, len(streams)):
        if j in began and not greeted:
            greeted = True
            peers = sum((pos[a] < dims[a] - 1).astype(jnp.int32)
                        + (pos[a] > 0).astype(jnp.int32) for a in axes)
            pl.semaphore_wait(barrier, peers)
        began.add(j)
        next(running[j], None)
    for end in ends:
        end()


def body(dims, global_weights, local_weights, momentum):
    layers, rows, width = global_weights.shape
    islands = lax.axis_size("island")
    cols = momentum.shape[2]
    groups = layers * rows // SUBLANES
    tiles = cols // LANES

    def to_tiles(array):
        array = array.reshape(groups, SUBLANES, -1, LANES)
        return array.transpose(0, 2, 1, 3)

    def from_tiles(array, like):
        array = array.reshape(groups, -1, SUBLANES, LANES)
        return array.transpose(0, 2, 1, 3).reshape(like.shape)

    wide = (groups,) + dims + (tiles, SUBLANES, LANES)
    narrow = (groups, tiles, SUBLANES, LANES)
    streams = plan(dims, groups)
    landings = []
    for order, _, ng in streams:
        left = dict(enumerate(dims))
        for a in order:
            n = left.pop(a)
            landings.append(pltpu.VMEM(
                (phase_slots(n), ng) + tuple(left[b] for b in sorted(left))
                + (tiles, SUBLANES, LANES), jnp.float32))
    n_sems = len(streams) * 4 * sum(n - 1 for n in dims)
    f32 = jnp.float32
    new_global, new_momentum = pl.pallas_call(
        functools.partial(kernel, dims, streams, n_sems),
        out_shape=(jax.ShapeDtypeStruct(wide, f32), jax.ShapeDtypeStruct(narrow, f32)),
        in_specs=[pl.BlockSpec(memory_space=pltpu.HBM)] * 3,
        out_specs=(pl.BlockSpec(memory_space=pl.ANY),) * 2,
        scratch_shapes=[
            pltpu.VMEM(wide, f32), pltpu.VMEM(wide, f32), pltpu.VMEM(narrow, f32),
            pltpu.VMEM(wide, f32), pltpu.VMEM(wide, f32), pltpu.VMEM(narrow, f32),
            landings,
            pltpu.SemaphoreType.DMA((n_sems,)), pltpu.SemaphoreType.DMA((n_sems,)),
            pltpu.SemaphoreType.DMA((3 * len(streams),)),
            pltpu.SemaphoreType.DMA((2 * len(streams),)),
        ],
        compiler_params=pltpu.CompilerParams(
            collective_id=0, has_side_effects=True, vmem_limit_bytes=40 * 2**20),
    )(
        to_tiles(global_weights).reshape(wide),
        to_tiles(local_weights[0]).reshape(wide),
        to_tiles(momentum),
    )
    return from_tiles(new_global, global_weights), from_tiles(new_momentum, momentum)


def solution(mesh):
    dims = grid_of(mesh.shape["island"])
    return jax.shard_map(
        functools.partial(body, dims),
        mesh=mesh,
        in_specs=(
            P(None, "fsdp", None),
            P("island", None, "fsdp", None),
            P(None, "fsdp", "island"),
        ),
        out_specs=(P(None, "fsdp", None), P(None, "fsdp", "island")),
        check_vma=False,
    )
```

```python
import functools

import jax
import jax.numpy as jnp
from jax import lax
from jax.experimental import pallas as pl
from jax.experimental.pallas import tpu as pltpu
from jax.sharding import PartitionSpec as P

NESTEROV = 0.9
OUTER_RATE = 0.7
ORDER = [2, 2, 6, 6, 0, 0, 1, 4, 1, 0, 5, 3, 0, 0, 3, 5, 7, 3, 6, 0, 3, 2, 7, 3, 5, 0, 6, 6, 4, 1, 3, 6, 6, 3, 2, 5, 5, 6, 2, 2, 7, 6, 5, 5, 0, 1, 1, 4, 2, 5, 6, 6, 2, 3, 5, 7, 1, 2, 7, 6, 6, 0, 5, 5, 3, 2, 4, 1, 4, 7, 7, 6, 0, 5, 5, 6, 1, 1, 4, 4, 0, 3, 5, 5, 2, 7, 1, 1, 4, 2, 6, 5, 4, 0, 7, 1, 2, 4, 1, 4, 2, 3, 7, 7, 5, 2, 0, 6, 1, 4, 1, 2, 7, 4, 7, 4, 1, 7, 0, 7, 3, 7, 4, 3, 4, 6, 2, 0, 1, 0, 4, 3, 3, 0, 5, 7, 3, 3, 1, 0, 3, 2, 4, 7]
LANES = 128
SUBLANES = 8


def grid_of(islands):
    return {16: (4, 2, 2), 64: (8, 8)}.get(islands, (islands,))


def plan(dims, groups):
    if len(dims) == 3:
        z, y, x = 0, 1, 2
        wish = [((0, 1, 2), 2), ((2, 1, 0), 2), ((1, 2, 0), 2), ((0, 2, 1), 2), ((2, 1, 0), 2), ((1, 2, 0), 2), ((2, 1, 0), 2), ((1, 2, 0), 2)]
    elif len(dims) == 2:
        wish = [((0, 1), 1), ((1, 0), 1)]
    else:
        wish = [((0,), 1)]
    total = sum(share for _, share in wish)
    streams, at, seen = [], 0, 0
    for order, share in wish:
        seen += share
        end = groups * seen // total
        if end > at:
            streams.append((order, at, end - at))
        at = end
    return streams


def turns(dims, n_streams):
    if ORDER is not None and len(dims) == 3:
        return ORDER
    steps = 2 + 2 * sum(1 if n == 2 else 2 * (n - 1) for n in dims)
    return [j for _ in range(steps) for j in range(n_streams)]


def phase_slots(n):
    return 1 if n == 2 else 2 * (n - 1)


def kernel(dims, streams, n_sems, g_hbm, l_hbm, m_hbm, out_hbm, nm_hbm,
           gw, lw, mom, acc, gath, nm, landing, send_sem, recv_sem, in_sem, out_sem):
    axes = range(len(dims))
    me = lax.axis_index("island")
    strides = []
    for a in axes:
        stride = 1
        for b in dims[a + 1:]:
            stride *= b
        strides.append(stride)
    pos = [(me // strides[a]) % dims[a] for a in axes]
    islands = strides[0] * dims[0]

    loads = []
    for j, (_, g0, ng) in enumerate(streams):
        rows = pl.ds(g0, ng)
        loads.append([
            pltpu.make_async_copy(g_hbm.at[rows], gw.at[rows], in_sem.at[3 * j]),
            pltpu.make_async_copy(l_hbm.at[rows], lw.at[rows], in_sem.at[3 * j + 1]),
            pltpu.make_async_copy(m_hbm.at[rows], mom.at[rows], in_sem.at[3 * j + 2]),
        ])
        for load in loads[-1][:2]:
            load.start()
    for load in loads:
        load[2].start()

    barrier = pltpu.get_barrier_semaphore()
    for a in axes:
        for step, there in ((1, pos[a] < dims[a] - 1), (-1, pos[a] > 0)):
            @pl.when(there)
            def _():
                pl.semaphore_signal(barrier, inc=1,
                                    device_id={"island": me + step * strides[a]},
                                    device_id_type=pl.DeviceIdType.MESH)

    counter = iter(range(n_sems))
    ends = []

    def remote(src, dst, sem, axis, step):
        return pltpu.make_async_remote_copy(
            src_ref=src, dst_ref=dst, send_sem=send_sem.at[sem],
            recv_sem=recv_sem.at[sem],
            device_id={"island": me + step * strides[axis]},
            device_id_type=pl.DeviceIdType.MESH)

    def part(ref, rows, fixed):
        return ref.at[(rows,) + tuple(fixed.get(a, slice(None)) for a in axes)]

    def stream(j):
        order, g0, ng = streams[j]
        rows = pl.ds(g0, ng)
        loads[j][0].wait()
        loads[j][1].wait()
        acc[rows] = gw[rows] - lw[rows]
        yield
        fixed = {}
        for phase, a in enumerate(order):
            n, p = dims[a], pos[a]
            land = landing[j * len(dims) + phase]
            sems = [[next(counter) for _ in range(n - 1)] for _ in range(2)]

            def slot(side, k, land=land, n=n):
                return land.at[0 if n == 2 else side * (n - 1) + k]

            def mine(s, a=a, fixed=dict(fixed)):
                return part(acc, rows, {**fixed, a: s})

            def take(side, k, s):
                block = mine(s)
                remote(block, slot(side, k), sems[side][k], a, 1 - 2 * side).wait_recv()
                block[...] = block[...] + slot(side, k)[...]

            for k in range(n - 1):
                for side in range(2):
                    lead = p if side == 0 else n - 1 - p
                    s = n - 1 - k + p if side == 0 else k - lead

                    @pl.when(lead <= k)
                    def _():
                        if k > 0:
                            @pl.when(lead > 0)
                            def _():
                                take(side, k - 1, s)
                        remote(mine(s), slot(side, k), sems[side][k], a,
                               1 - 2 * side).start()

                    def end(lead=lead, k=k, side=side, s=s, a=a,
                            mine=mine, slot=slot, sems=sems):
                        @pl.when(lead <= k)
                        def _():
                            remote(mine(s), slot(side, k), sems[side][k], a,
                                   1 - 2 * side).wait_send()
                    ends.append(end)
                    if n > 2 or side == 1:
                        yield
            for side in range(2):
                @pl.when((p if side == 0 else n - 1 - p) > 0)
                def _():
                    take(side, n - 2, p)
            fixed[a] = p

        own = (rows,) + tuple(pos)
        loads[j][2].wait()
        outer = acc[own] / islands
        moment = NESTEROV * mom[rows] + outer
        nm[rows] = moment
        gath[own] = gw[own] - OUTER_RATE * (outer + NESTEROV * moment)
        save = pltpu.make_async_copy(nm.at[rows], nm_hbm.at[rows], out_sem.at[2 * j])
        save.start()
        ends.append(save.wait)

        for a in reversed(order):
            n, p = dims[a], pos[a]
            del fixed[a]
            sems = [[next(counter) for _ in range(n - 1)] for _ in range(2)]

            def block_of(s, a=a, fixed=dict(fixed)):
                return part(gath, rows, {**fixed, a: s})

            for k in range(n):
                for side in range(2):
                    step = 1 - 2 * side
                    lead = p if side == 0 else n - 1 - p
                    s = p - step * k

                    @pl.when(k <= lead)
                    def _():
                        block = block_of(s)
                        if k > 0:
                            remote(block, block, sems[side][k - 1], a, step).wait_recv()
                        if k < n - 1:
                            @pl.when(lead < n - 1)
                            def _():
                                remote(block, block, sems[side][k], a, step).start()

                    if k < n - 1:
                        def end(k=k, lead=lead, n=n, s=s, side=side, step=step, a=a,
                                block_of=block_of, sems=sems):
                            @pl.when((k <= lead) & (lead < n - 1))
                            def _():
                                block = block_of(s)
                                remote(block, block, sems[side][k], a, step).wait_send()
                        ends.append(end)
                        if n > 2 or side == 1:
                            yield
        store = pltpu.make_async_copy(gath.at[rows], out_hbm.at[rows], out_sem.at[2 * j + 1])
        store.start()
        ends.append(store.wait)

    running = [stream(j) for j in range(len(streams))]
    greeted = False
    began = set()
    for j in turns(dims, len(streams)):
        if j in began and not greeted:
            greeted = True
            peers = sum((pos[a] < dims[a] - 1).astype(jnp.int32)
                        + (pos[a] > 0).astype(jnp.int32) for a in axes)
            pl.semaphore_wait(barrier, peers)
        began.add(j)
        next(running[j], None)
    for end in ends:
        end()


def body(dims, global_weights, local_weights, momentum):
    layers, rows, width = global_weights.shape
    islands = lax.axis_size("island")
    cols = momentum.shape[2]
    groups = layers * rows // SUBLANES
    tiles = cols // LANES

    def to_tiles(array):
        array = array.reshape(groups, SUBLANES, -1, LANES)
        return array.transpose(0, 2, 1, 3)

    def from_tiles(array, like):
        array = array.reshape(groups, -1, SUBLANES, LANES)
        return array.transpose(0, 2, 1, 3).reshape(like.shape)

    wide = (groups,) + dims + (tiles, SUBLANES, LANES)
    narrow = (groups, tiles, SUBLANES, LANES)
    streams = plan(dims, groups)
    landings = []
    for order, _, ng in streams:
        left = dict(enumerate(dims))
        for a in order:
            n = left.pop(a)
            landings.append(pltpu.VMEM(
                (phase_slots(n), ng) + tuple(left[b] for b in sorted(left))
                + (tiles, SUBLANES, LANES), jnp.float32))
    n_sems = len(streams) * 4 * sum(n - 1 for n in dims)
    f32 = jnp.float32
    new_global, new_momentum = pl.pallas_call(
        functools.partial(kernel, dims, streams, n_sems),
        out_shape=(jax.ShapeDtypeStruct(wide, f32), jax.ShapeDtypeStruct(narrow, f32)),
        in_specs=[pl.BlockSpec(memory_space=pltpu.HBM)] * 3,
        out_specs=(pl.BlockSpec(memory_space=pl.ANY),) * 2,
        scratch_shapes=[
            pltpu.VMEM(wide, f32), pltpu.VMEM(wide, f32), pltpu.VMEM(narrow, f32),
            pltpu.VMEM(wide, f32), pltpu.VMEM(wide, f32), pltpu.VMEM(narrow, f32),
            landings,
            pltpu.SemaphoreType.DMA((n_sems,)), pltpu.SemaphoreType.DMA((n_sems,)),
            pltpu.SemaphoreType.DMA((3 * len(streams),)),
            pltpu.SemaphoreType.DMA((2 * len(streams),)),
        ],
        compiler_params=pltpu.CompilerParams(
            collective_id=0, has_side_effects=True, vmem_limit_bytes=40 * 2**20),
    )(
        to_tiles(global_weights).reshape(wide),
        to_tiles(local_weights[0]).reshape(wide),
        to_tiles(momentum),
    )
    return from_tiles(new_global, global_weights), from_tiles(new_momentum, momentum)


def solution(mesh):
    dims = grid_of(mesh.shape["island"])
    return jax.shard_map(
        functools.partial(body, dims),
        mesh=mesh,
        in_specs=(
            P(None, "fsdp", None),
            P("island", None, "fsdp", None),
            P(None, "fsdp", "island"),
        ),
        out_specs=(P(None, "fsdp", None), P(None, "fsdp", "island")),
        check_vma=False,
    )
```

```python
import functools

import jax
import jax.numpy as jnp
from jax import lax
from jax.experimental import pallas as pl
from jax.experimental.pallas import tpu as pltpu
from jax.sharding import PartitionSpec as P

NESTEROV = 0.9
OUTER_RATE = 0.7
ORDER = [2, 2, 6, 6, 0, 0, 1, 4, 1, 0, 5, 3, 0, 0, 3, 5, 7, 3, 6, 0, 3, 2, 7, 3, 5, 0, 6, 6, 4, 1, 3, 6, 6, 3, 2, 5, 5, 6, 2, 2, 7, 6, 5, 5, 0, 1, 1, 4, 2, 5, 6, 6, 2, 3, 5, 7, 1, 2, 7, 6, 6, 0, 5, 5, 3, 2, 4, 1, 4, 7, 7, 6, 0, 5, 5, 6, 1, 1, 4, 4, 0, 3, 5, 5, 2, 7, 1, 1, 4, 2, 6, 5, 4, 0, 7, 1, 2, 4, 1, 4, 2, 3, 7, 7, 5, 2, 0, 6, 1, 4, 1, 2, 7, 4, 7, 4, 1, 7, 0, 7, 3, 7, 4, 3, 4, 6, 2, 0, 1, 0, 4, 3, 3, 0, 5, 7, 3, 3, 1, 0, 3, 2, 4, 7]
LANES = 128
SUBLANES = 8


def grid_of(islands):
    return {16: (4, 2, 2), 64: (8, 8)}.get(islands, (islands,))


def plan(dims, groups):
    if len(dims) == 3:
        z, y, x = 0, 1, 2
        wish = [((0, 1, 2), 2), ((2, 1, 0), 2), ((1, 2, 0), 2), ((0, 2, 1), 2), ((2, 1, 0), 2), ((1, 2, 0), 2), ((2, 1, 0), 2), ((1, 2, 0), 2)]
    elif len(dims) == 2:
        wish = [((0, 1), 1), ((1, 0), 1)]
    else:
        wish = [((0,), 1)]
    total = sum(share for _, share in wish)
    streams, at, seen = [], 0, 0
    for order, share in wish:
        seen += share
        end = groups * seen // total
        if end > at:
            streams.append((order, at, end - at))
        at = end
    return streams


def turns(dims, n_streams):
    if ORDER is not None and len(dims) == 3:
        return ORDER
    steps = 2 + 2 * sum(1 if n == 2 else 2 * (n - 1) for n in dims)
    return [j for _ in range(steps) for j in range(n_streams)]


def phase_slots(n):
    return 1 if n == 2 else 2 * (n - 1)


def kernel(dims, streams, n_sems, gw, lw, mom, out_hbm, nm_hbm,
           acc, gath, nm, landing, send_sem, recv_sem, out_sem):
    axes = range(len(dims))
    me = lax.axis_index("island")
    strides = []
    for a in axes:
        stride = 1
        for b in dims[a + 1:]:
            stride *= b
        strides.append(stride)
    pos = [(me // strides[a]) % dims[a] for a in axes]
    islands = strides[0] * dims[0]

    barrier = pltpu.get_barrier_semaphore()
    for a in axes:
        for step, there in ((1, pos[a] < dims[a] - 1), (-1, pos[a] > 0)):
            @pl.when(there)
            def _():
                pl.semaphore_signal(barrier, inc=1,
                                    device_id={"island": me + step * strides[a]},
                                    device_id_type=pl.DeviceIdType.MESH)

    counter = iter(range(n_sems))
    ends = []

    def remote(src, dst, sem, axis, step):
        return pltpu.make_async_remote_copy(
            src_ref=src, dst_ref=dst, send_sem=send_sem.at[sem],
            recv_sem=recv_sem.at[sem],
            device_id={"island": me + step * strides[axis]},
            device_id_type=pl.DeviceIdType.MESH)

    def part(ref, rows, fixed):
        return ref.at[(rows,) + tuple(fixed.get(a, slice(None)) for a in axes)]

    def stream(j):
        order, g0, ng = streams[j]
        rows = pl.ds(g0, ng)
        acc[rows] = gw[rows] - lw[rows]
        yield
        fixed = {}
        for phase, a in enumerate(order):
            n, p = dims[a], pos[a]
            land = landing[j * len(dims) + phase]
            sems = [[next(counter) for _ in range(n - 1)] for _ in range(2)]

            def slot(side, k, land=land, n=n):
                return land.at[0 if n == 2 else side * (n - 1) + k]

            def mine(s, a=a, fixed=dict(fixed)):
                return part(acc, rows, {**fixed, a: s})

            def take(side, k, s):
                block = mine(s)
                remote(block, slot(side, k), sems[side][k], a, 1 - 2 * side).wait_recv()
                block[...] = block[...] + slot(side, k)[...]

            for k in range(n - 1):
                for side in range(2):
                    lead = p if side == 0 else n - 1 - p
                    s = n - 1 - k + p if side == 0 else k - lead

                    @pl.when(lead <= k)
                    def _():
                        if k > 0:
                            @pl.when(lead > 0)
                            def _():
                                take(side, k - 1, s)
                        remote(mine(s), slot(side, k), sems[side][k], a,
                               1 - 2 * side).start()

                    def end(lead=lead, k=k, side=side, s=s, a=a,
                            mine=mine, slot=slot, sems=sems):
                        @pl.when(lead <= k)
                        def _():
                            remote(mine(s), slot(side, k), sems[side][k], a,
                                   1 - 2 * side).wait_send()
                    ends.append(end)
                    if n > 2 or side == 1:
                        yield
            for side in range(2):
                @pl.when((p if side == 0 else n - 1 - p) > 0)
                def _():
                    take(side, n - 2, p)
            fixed[a] = p

        own = (rows,) + tuple(pos)
        outer = acc[own] / islands
        moment = NESTEROV * mom[rows] + outer
        nm[rows] = moment
        gath[own] = gw[own] - OUTER_RATE * (outer + NESTEROV * moment)
        save = pltpu.make_async_copy(nm.at[rows], nm_hbm.at[rows], out_sem.at[2 * j])
        save.start()
        ends.append(save.wait)

        for a in reversed(order):
            n, p = dims[a], pos[a]
            del fixed[a]
            sems = [[next(counter) for _ in range(n - 1)] for _ in range(2)]

            def block_of(s, a=a, fixed=dict(fixed)):
                return part(gath, rows, {**fixed, a: s})

            for k in range(n):
                for side in range(2):
                    step = 1 - 2 * side
                    lead = p if side == 0 else n - 1 - p
                    s = p - step * k

                    @pl.when(k <= lead)
                    def _():
                        block = block_of(s)
                        if k > 0:
                            remote(block, block, sems[side][k - 1], a, step).wait_recv()
                        if k < n - 1:
                            @pl.when(lead < n - 1)
                            def _():
                                remote(block, block, sems[side][k], a, step).start()

                    if k < n - 1:
                        def end(k=k, lead=lead, n=n, s=s, side=side, step=step, a=a,
                                block_of=block_of, sems=sems):
                            @pl.when((k <= lead) & (lead < n - 1))
                            def _():
                                block = block_of(s)
                                remote(block, block, sems[side][k], a, step).wait_send()
                        ends.append(end)
                        if n > 2 or side == 1:
                            yield
        store = pltpu.make_async_copy(gath.at[rows], out_hbm.at[rows], out_sem.at[2 * j + 1])
        store.start()
        ends.append(store.wait)

    running = [stream(j) for j in range(len(streams))]
    greeted = False
    began = set()
    for j in turns(dims, len(streams)):
        if j in began and not greeted:
            greeted = True
            peers = sum((pos[a] < dims[a] - 1).astype(jnp.int32)
                        + (pos[a] > 0).astype(jnp.int32) for a in axes)
            pl.semaphore_wait(barrier, peers)
        began.add(j)
        next(running[j], None)
    for end in ends:
        end()


def body(dims, global_weights, local_weights, momentum):
    layers, rows, width = global_weights.shape
    islands = lax.axis_size("island")
    cols = momentum.shape[2]
    groups = layers * rows // SUBLANES
    tiles = cols // LANES

    def to_tiles(array):
        array = array.reshape(groups, SUBLANES, -1, LANES)
        return array.transpose(0, 2, 1, 3)

    def from_tiles(array, like):
        array = array.reshape(groups, -1, SUBLANES, LANES)
        return array.transpose(0, 2, 1, 3).reshape(like.shape)

    wide = (groups,) + dims + (tiles, SUBLANES, LANES)
    narrow = (groups, tiles, SUBLANES, LANES)
    streams = plan(dims, groups)
    landings = []
    for order, _, ng in streams:
        left = dict(enumerate(dims))
        for a in order:
            n = left.pop(a)
            landings.append(pltpu.VMEM(
                (phase_slots(n), ng) + tuple(left[b] for b in sorted(left))
                + (tiles, SUBLANES, LANES), jnp.float32))
    n_sems = len(streams) * 4 * sum(n - 1 for n in dims)
    f32 = jnp.float32
    new_global, new_momentum = pl.pallas_call(
        functools.partial(kernel, dims, streams, n_sems),
        out_shape=(jax.ShapeDtypeStruct(wide, f32), jax.ShapeDtypeStruct(narrow, f32)),
        in_specs=[pl.BlockSpec(memory_space=pltpu.VMEM)] * 3,
        out_specs=(pl.BlockSpec(memory_space=pl.ANY),) * 2,
        scratch_shapes=[
            pltpu.VMEM(wide, f32), pltpu.VMEM(wide, f32), pltpu.VMEM(narrow, f32),
            landings,
            pltpu.SemaphoreType.DMA((n_sems,)), pltpu.SemaphoreType.DMA((n_sems,)),
            pltpu.SemaphoreType.DMA((2 * len(streams),)),
        ],
        compiler_params=pltpu.CompilerParams(
            collective_id=0, has_side_effects=True, vmem_limit_bytes=40 * 2**20),
    )(
        to_tiles(global_weights).reshape(wide),
        to_tiles(local_weights[0]).reshape(wide),
        to_tiles(momentum),
    )
    return from_tiles(new_global, global_weights), from_tiles(new_momentum, momentum)


def solution(mesh):
    dims = grid_of(mesh.shape["island"])
    return jax.shard_map(
        functools.partial(body, dims),
        mesh=mesh,
        in_specs=(
            P(None, "fsdp", None),
            P("island", None, "fsdp", None),
            P(None, "fsdp", "island"),
        ),
        out_specs=(P(None, "fsdp", None), P(None, "fsdp", "island")),
        check_vma=False,
    )
```
